32 devices in a mesh: seq: 16 (over z, y, core), head: 2 (over x).
Axes of the slice: x: 2, y: 2, z: 4, core: 2. Of those that a mesh axis runs over, the one named last changes fastest.
Arguments:
- queries: bfloat16 [6144, 3072], P('seq', 'head')
- keys: bfloat16 [6144, 3072], P('seq', 'head')
- values: bfloat16 [6144, 3072], P('seq', 'head'), may hold values from -6 to 6
- kv_tiles: int32 [16, 13], replicated, may hold values from -1 to 15, as said below
- tile_order: int32 [16], replicated, may hold values from 0 to 15, as said below
- out_weight: bfloat16 [3072, 3072], P('head'), may hold values from -0.109375 to 0.109375
Outputs:
- projected: bfloat16 [6144, 3072], P('seq', 'head')
The draws below stay inside these ranges and needn't reach their ends.
Inputs may be any that keep to these rules, and one draw needn't show every extreme that they name: tile_order is a rotation: slot p holds tile (p + c) mod 16 for one c. `kv_tiles`: row t lists distinct tiles in increasing order, then -1 entries; it always holds t; every listed u has |u - t| <= 6; t - 6 and t + 6 are listed wherever they are tiles.
All inputs are finite; a program needn't handle non-finite values.
Results may differ from the reference program's by a relative error of at most 0.014.
Values may be sent and summed in bfloat16 or wider, within the bound.
A program may use at most 256 MiB of HBM per device.

```python
import math
import jax
import jax.numpy as jnp
from jax import lax

D = 3072
HEADS = 24
HEAD_DIM = 128
TILE = 384
REACH = 6
TILES = 16
KMAX = 13
TOKENS = 6144
N_HEAD = 2


def drawn_pair(key):
    base_queries = jax.random.normal(jax.random.fold_in(key, 101), (TOKENS, D), jnp.float32)
    base_keys = jax.random.normal(jax.random.fold_in(key, 102), (TOKENS, D), jnp.float32)
    return (base_queries, base_keys)


def draw_queries(key, part):
    return drawn_pair(key)[0].astype(jnp.bfloat16)


def draw_keys(key, part):
    return drawn_pair(key)[1].astype(jnp.bfloat16)


def draw_kv_tiles(key, part):
    tile_ids = jnp.arange(TILES, dtype=jnp.int32)[:, None]
    offsets = jnp.arange(KMAX, dtype=jnp.int32)[None, :] - REACH
    candidate = tile_ids + offsets
    inside = (candidate >= 0) & (candidate < TILES)
    coins = jax.random.randint(key, (TILES, KMAX), 0, 4)
    chosen = inside & ((coins > 0) | (offsets == 0) | (jnp.abs(offsets) == REACH))
    ranking = jnp.where(chosen, offsets + REACH, offsets + REACH + KMAX)
    arrangement = jnp.argsort(ranking, axis=1, stable=True)
    packed = jnp.take_along_axis(candidate, arrangement, axis=1)
    kept = jnp.take_along_axis(chosen, arrangement, axis=1)
    return jnp.where(kept, packed, -1).astype(jnp.int32)


def draw_tile_order(key, part):
    start = jax.random.randint(key, (), 0, TILES)
    return ((jnp.arange(TILES, dtype=jnp.int32) + start) % TILES).astype(jnp.int32)


def steps_of(key, shape, pieces, least, largest):
    level = 1.0
    for dim, parts in pieces:
        steps = jax.random.uniform(jax.random.fold_in(jax.random.fold_in(key, 6), dim), (parts,), jnp.float32, least / len(pieces), largest / len(pieces))
        level = level * jnp.repeat(jnp.exp(steps), shape[dim] // parts).reshape((-1,) + (1,) * (len(shape) - 1 - dim))
    return level


def normal_values(own_key, shape, spread, limit, pieces=(), held_as=jnp.bfloat16):
    level = steps_of(own_key, shape, pieces, -0.22, 0.18) if pieces else 1.0
    drawn = jax.random.normal(own_key, shape, jnp.float32) * spread * level
    return jnp.minimum(jnp.maximum(drawn, -limit), limit).astype(held_as)


def setup_inputs(seed: int = 0) -> dict:
    splits = jax.random.split(jax.random.key(seed), 7)
    return {
        "queries": draw_queries(jax.random.fold_in(splits[6], 71), 0),
        "keys": draw_keys(jax.random.fold_in(splits[6], 71), 0),
        "values": normal_values(splits[2], (TOKENS, D), 1.0, 6.0, ((0, 16), (1, 2))),
        "kv_tiles": draw_kv_tiles(jax.random.fold_in(splits[6], 71), 0),
        "tile_order": draw_tile_order(jax.random.fold_in(splits[6], 71), 0),
        "out_weight": normal_values(splits[5], (D, D), D ** -0.5, 0.109375, ((0, 2),)),
    }


def reference(queries, keys, values, kv_tiles, tile_order, out_weight):
    slot_ids = jnp.arange(TILES, dtype=jnp.int32)
    slot_of = jnp.zeros((TILES,), jnp.int32).at[tile_order].set(slot_ids)
    query_tiles = queries.reshape(TILES, TILE, HEADS, HEAD_DIM)
    key_tiles = keys.reshape(TILES, TILE, HEADS, HEAD_DIM)
    value_tiles = values.reshape(TILES, TILE, HEADS, HEAD_DIM)
    score_scale = 1.0 / math.sqrt(HEAD_DIM)

    def one_slot(slot_index):
        listed = kv_tiles[tile_order[slot_index]]
        present = listed >= 0
        source = slot_of[jnp.maximum(listed, 0)]
        key_rows = key_tiles[source].astype(jnp.float32)
        value_rows = value_tiles[source].astype(jnp.float32)
        query_rows = query_tiles[slot_index].astype(jnp.float32)
        scores = jnp.einsum('qhd,jkhd->hqjk', query_rows, key_rows) * score_scale
        allowed = present[None, None, :, None]
        top_score = lax.optimization_barrier(jnp.max(jnp.where(allowed, scores, -jnp.inf), axis=(2, 3)))
        exponent = jnp.where(allowed, jnp.exp(scores - top_score[:, :, None, None]), 0.0)
        denominator = lax.optimization_barrier(jnp.sum(exponent, axis=(2, 3)))
        weights = lax.optimization_barrier(exponent.astype(jnp.bfloat16)).astype(jnp.float32)
        summed = jnp.einsum('hqjk,jkhd->qhd', weights, value_rows)
        attended_tile = summed / jnp.transpose(denominator)[:, :, None]
        return attended_tile.astype(jnp.bfloat16).reshape(TILE, D)
    attended = lax.map(one_slot, slot_ids).reshape(TOKENS, D)
    group_width = D // N_HEAD
    result = jnp.zeros((TOKENS, D), jnp.float32)
    for group_index in range(N_HEAD):
        lower = group_index * group_width
        group_term = jnp.dot(attended[:, lower:lower + group_width], out_weight[lower:lower + group_width], preferred_element_type=jnp.float32).astype(jnp.bfloat16)
        group_term = lax.optimization_barrier(group_term)
        result = result + group_term.astype(jnp.float32)
    return result.astype(jnp.bfloat16)
```

```python
import functools
import math

import jax
import jax.numpy as jnp
from jax import lax
from jax.experimental import pallas as pl
from jax.experimental.pallas import tpu as pltpu
from jax.sharding import PartitionSpec as P

HEAD_DIM = 128
REACH = 6


def attention_body(width, place_ref, count_ref, q_ref, k_ref, v_ref, out_ref, scores, tops):
    row = pl.program_id(1)
    count = count_ref[row]
    query = q_ref[0, 0]
    tile_rows = query.shape[0]
    scale = math.log2(math.e) / math.sqrt(HEAD_DIM)
    tops[...] = jnp.full(tops.shape, -jnp.inf, jnp.float32)

    def find(entry, carry):
        place = place_ref[row * width + entry]
        fresh = lax.dot_general(
            query, k_ref[0, place], (((1,), (1,)), ((), ())), preferred_element_type=jnp.float32
        )
        scores[entry] = fresh
        best = tops[...]
        for lane in range(0, fresh.shape[1], HEAD_DIM):
            best = jnp.maximum(best, fresh[:, lane : lane + HEAD_DIM])
        tops[...] = best
        return carry

    lax.fori_loop(0, count, find, 0)
    top = jnp.max(tops[...], axis=1, keepdims=True) * scale
    ones = jnp.ones((k_ref.shape[2], HEAD_DIM), jnp.bfloat16)

    def add(entry, summed):
        place = place_ref[row * width + entry]
        weights = jnp.exp2(scores[entry] * scale - top).astype(jnp.bfloat16)
        paired = jnp.concatenate([v_ref[0, place], ones], axis=1)
        return summed + jnp.dot(weights, paired, preferred_element_type=jnp.float32)

    summed = lax.fori_loop(0, count, add, jnp.zeros((tile_rows, 2 * HEAD_DIM), jnp.float32))
    out_ref[0, 0] = (summed[:, :HEAD_DIM] / summed[:, HEAD_DIM:]).astype(jnp.bfloat16)


def attention(q, k, v, place, count):
    heads, query_tiles, rows, _ = q.shape
    key_tiles = k.shape[1]
    width = place.shape[1]
    units = heads * query_tiles * min(width, key_tiles)
    key_spec = pl.BlockSpec((1, key_tiles, rows, HEAD_DIM), lambda h, t, *_: (h, 0, 0, 0))
    tile_spec = pl.BlockSpec((1, 1, rows, HEAD_DIM), lambda h, t, *_: (h, t, 0, 0))
    return pl.pallas_call(
        functools.partial(attention_body, width),
        out_shape=jax.ShapeDtypeStruct(q.shape, jnp.bfloat16),
        grid_spec=pltpu.PrefetchScalarGridSpec(
            num_scalar_prefetch=2,
            grid=(heads, query_tiles),
            in_specs=[tile_spec, key_spec, key_spec],
            out_specs=tile_spec,
            scratch_shapes=[
                pltpu.VMEM((width, rows, rows), jnp.float32),
                pltpu.VMEM((rows, HEAD_DIM), jnp.float32),
            ],
        ),
        compiler_params=pltpu.CompilerParams(vmem_limit_bytes=40 * 1024 * 1024),
        cost_estimate=pl.CostEstimate(
            flops=units * rows * rows * HEAD_DIM * 4,
            bytes_accessed=2 * (2 * q.size + k.size + v.size),
            transcendentals=units * rows * rows,
        ),
    )(place.reshape(-1), count, q, k, v)


def listed_slots(kv_tiles, tile_order, slot):
    listed = kv_tiles[tile_order[slot]]
    slot_ids = jnp.arange(tile_order.shape[0], dtype=jnp.int32)
    found = jnp.sum(
        jnp.where(tile_order[None, :] == jnp.maximum(listed, 0)[:, None], slot_ids[None, :], 0), axis=1
    )
    return found, jnp.sum((listed >= 0).astype(jnp.int32))


def by_ring(queries, keys, values, kv_tiles, tile_order, out_weight):
    rows, local_width = queries.shape
    heads = local_width // HEAD_DIM
    n = lax.axis_size("seq")
    me = lax.axis_index("seq")
    window = 2 * REACH + 1
    pair = jnp.stack([keys, values])
    received = {0: pair}
    for heading in (1, -1):
        moving = pair
        for stride in range(1, REACH + 1):
            moving = lax.ppermute(moving, "seq", [(i, (i + heading) % n) for i in range(n)])
            received[-heading * stride] = moving
    both = jnp.stack([received[o] for o in range(-REACH, REACH + 1)])
    both = both.reshape(window, 2, rows, heads, HEAD_DIM).transpose(1, 3, 0, 2, 4)
    q = queries.reshape(rows, heads, HEAD_DIM).transpose(1, 0, 2)[:, None]
    slots, count = listed_slots(kv_tiles, tile_order, me)
    place = (slots - me + REACH) % n
    place = jnp.clip(place, 0, window - 1)
    attended = attention(q, both[0], both[1], place[None], count[None])
    attended = attended[:, 0].transpose(1, 0, 2).reshape(rows, local_width)
    partial = jnp.dot(attended, out_weight, preferred_element_type=jnp.float32).astype(jnp.bfloat16)
    return lax.psum_scatter(partial, "head", scatter_dimension=1, tiled=True)


def by_heads(groups, queries, keys, values, kv_tiles, tile_order, out_weight):
    rows, local_width = queries.shape
    heads = local_width // HEAD_DIM
    n = lax.axis_size("seq")
    n_head = lax.axis_size("head")
    sub = n // groups
    share = heads // groups
    me = lax.axis_index("seq")
    plane, inner = me // sub, me % sub

    def plane_shift(x, by):
        return lax.ppermute(
            x, "seq", [(i, (i // sub + by) % groups * sub + i % sub) for i in range(n)]
        )

    def inner_swap(x, bit):
        return lax.ppermute(x, "seq", [(i, i ^ bit) for i in range(n)])

    bits = []
    bit = sub // 2
    while bit:
        bits.append(bit)
        bit //= 2
    mask_place = [0] * sub
    for mask in range(sub):
        mask_place[mask] = sum(1 << i for i, b in enumerate(bits) if mask & b)
    mask_place = jnp.array(mask_place, jnp.int32)

    def place_of(slot):
        return mask_place[(slot % sub) ^ inner] * groups + (plane - slot // sub) % groups

    places, counts = [], []
    for o in range(groups):
        slots, count = listed_slots(kv_tiles, tile_order, (plane - o) % groups * sub + inner)
        places.append(place_of(slots))
        counts.append(count)
    place, count = jnp.stack(places), jnp.stack(counts)

    my_head = lax.axis_index("head")
    columns = out_weight.shape[1] // n_head
    half = out_weight.shape[0] // 2
    own_half = me % 2
    weight_rows = {0: lax.dynamic_slice_in_dim(out_weight, my_head * columns, columns, 1)}
    for o in range(1, n_head):
        piece = lax.dynamic_slice(
            out_weight, (own_half * half, (my_head + o) % n_head * columns), (half, columns)
        )
        piece = lax.ppermute(piece, "head", [(i, (i + o) % n_head) for i in range(n_head)])
        other = inner_swap(piece, 1)
        weight_rows[o] = jnp.where(
            own_half == 0,
            jnp.concatenate([piece, other], axis=0),
            jnp.concatenate([other, piece], axis=0),
        )

    def cut(array, to_plane, j):
        return lax.dynamic_slice_in_dim(array, (to_plane * share + j) * HEAD_DIM, HEAD_DIM, 1)

    total = jnp.zeros((rows, columns), jnp.float32)
    sent_before = None
    home = [[None] * groups for _ in range(share)]
    for j in range(share):
        pieces = []
        for o in range(groups):
            to_plane = (plane + o) % groups
            pieces.append(jnp.stack([cut(a, to_plane, j) for a in (queries, keys, values)]))
        if sent_before is not None:
            pieces, sent_before = lax.optimization_barrier((pieces, sent_before))
        arrived = [pieces[0]] + [plane_shift(pieces[o], o) for o in range(1, groups)]
        sent_before = arrived
        stacked = jnp.stack(arrived)
        q = stacked[:, 0][None]
        both = stacked[:, 1:].transpose(1, 0, 2, 3)
        for b in bits:
            both = jnp.concatenate([both, inner_swap(both, b)], axis=1)
        attended = attention(q, both[0][None], both[1][None], place, count)[0]
        for o in range(groups):
            home[j][o] = attended[o] if o == 0 else plane_shift(attended[o], -o)
    for j in range(share):
        terms, weights = [], []
        for h in range(n_head):
            for o in range(groups):
                piece = home[j][o]
                if h:
                    piece = lax.ppermute(
                        piece, "head", [(i, (i + h) % n_head) for i in range(n_head)]
                    )
                terms.append(piece)
                start = ((plane + o) % groups * share + j) * HEAD_DIM
                weights.append(lax.dynamic_slice_in_dim(weight_rows[h], start, HEAD_DIM, 0))
        total = total + jnp.dot(
            jnp.concatenate(terms, axis=1),
            jnp.concatenate(weights, axis=0),
            preferred_element_type=jnp.float32,
        )
    return total.astype(jnp.bfloat16)


def per_device(queries, keys, values, kv_tiles, tile_order, out_weight):
    n = lax.axis_size("seq")
    groups = math.gcd(queries.shape[1] // HEAD_DIM, n)
    sub = n // groups
    power_of_two = sub & (sub - 1) == 0
    if groups > 1 and sub > 1 and power_of_two and n <= 2 * (2 * REACH + 1):
        return by_heads(groups, queries, keys, values, kv_tiles, tile_order, out_weight)
    return by_ring(queries, keys, values, kv_tiles, tile_order, out_weight)


def solution(mesh):
    return jax.shard_map(
        per_device,
        mesh=mesh,
        in_specs=(P("seq", "head"), P("seq", "head"), P("seq", "head"), P(), P(), P("head", None)),
        out_specs=P("seq", "head"),
        check_vma=False,
    )
```

```python
import functools
import math

import jax
import jax.numpy as jnp
from jax import lax
from jax.experimental import pallas as pl
from jax.experimental.pallas import tpu as pltpu
from jax.sharding import PartitionSpec as P

HEAD_DIM = 128
REACH = 6
MESH = pl.DeviceIdType.MESH


def attention_body(width, place_ref, count_ref, q_ref, k_ref, v_ref, out_ref, scores, tops, summed):
    row = pl.program_id(0)
    count = count_ref[row]
    heads = q_ref.shape[0]
    scale = math.log2(math.e) / math.sqrt(HEAD_DIM)
    tops[...] = jnp.full(tops.shape, -jnp.inf, jnp.float32)
    summed[...] = jnp.zeros(summed.shape, jnp.float32)
    ones = jnp.ones((k_ref.shape[2], HEAD_DIM), jnp.bfloat16)

    def find(entry, carry):
        place = place_ref[row * width + entry]
        for h in range(heads):
            fresh = lax.dot_general(
                q_ref[h, 0],
                k_ref[h, place],
                (((1,), (1,)), ((), ())),
                preferred_element_type=jnp.float32,
            )
            scores[h, entry] = fresh
            best = tops[h]
            for lane in range(0, fresh.shape[1], HEAD_DIM):
                best = jnp.maximum(best, fresh[:, lane : lane + HEAD_DIM])
            tops[h] = best
        return carry

    lax.fori_loop(0, count, find, 0)
    for h in range(heads):
        top = jnp.max(tops[h], axis=1, keepdims=True) * scale
        tops[h] = jnp.broadcast_to(top, tops.shape[1:])

    def add(entry, carry):
        place = place_ref[row * width + entry]
        for h in range(heads):
            weights = jnp.exp2(scores[h, entry] * scale - tops[h][:, :1]).astype(jnp.bfloat16)
            paired = jnp.concatenate([v_ref[h, place], ones], axis=1)
            summed[h] += jnp.dot(weights, paired, preferred_element_type=jnp.float32)
        return carry

    lax.fori_loop(0, count, add, 0)
    for h in range(heads):
        done = summed[h]
        out_ref[0, :, h * HEAD_DIM : (h + 1) * HEAD_DIM] = (
            done[:, :HEAD_DIM] / done[:, HEAD_DIM:]
        ).astype(jnp.bfloat16)


def attention(q, k, v, place, count, first, tiles):
    heads, _, rows, _ = q.shape
    key_tiles = k.shape[1]
    width = place.shape[1]
    units = heads * tiles * min(width, key_tiles)
    key_spec = pl.BlockSpec(
        (heads, key_tiles, rows, HEAD_DIM), lambda t, *_: (0, 0, 0, 0), pipeline_mode=pl.Buffered(1)
    )
    return pl.pallas_call(
        functools.partial(attention_body, width),
        out_shape=jax.ShapeDtypeStruct((tiles, rows, heads * HEAD_DIM), jnp.bfloat16),
        grid_spec=pltpu.PrefetchScalarGridSpec(
            num_scalar_prefetch=2,
            grid=(tiles,),
            in_specs=[
                pl.BlockSpec((heads, 1, rows, HEAD_DIM), lambda t, *_: (0, first + t, 0, 0)),
                key_spec,
                key_spec,
            ],
            out_specs=pl.BlockSpec((1, rows, heads * HEAD_DIM), lambda t, *_: (t, 0, 0)),
            scratch_shapes=[
                pltpu.VMEM((heads, width, rows, rows), jnp.float32),
                pltpu.VMEM((heads, rows, HEAD_DIM), jnp.float32),
                pltpu.VMEM((heads, rows, 2 * HEAD_DIM), jnp.float32),
            ],
        ),
        compiler_params=pltpu.CompilerParams(vmem_limit_bytes=52 * 1024 * 1024),
        cost_estimate=pl.CostEstimate(
            flops=units * rows * rows * HEAD_DIM * 4,
            bytes_accessed=2 * (2 * q.size + k.size + v.size),
            transcendentals=units * rows * rows,
        ),
    )(place[first : first + tiles].reshape(-1), count[first : first + tiles], q, k, v)


def listed_slots(kv_tiles, tile_order, slot):
    listed = kv_tiles[tile_order[slot]]
    slot_ids = jnp.arange(tile_order.shape[0], dtype=jnp.int32)
    found = jnp.sum(
        jnp.where(tile_order[None, :] == jnp.maximum(listed, 0)[:, None], slot_ids[None, :], 0), axis=1
    )
    return found, jnp.sum((listed >= 0).astype(jnp.int32))


def by_ring(queries, keys, values, kv_tiles, tile_order, out_weight):
    rows, local_width = queries.shape
    heads = local_width // HEAD_DIM
    n = lax.axis_size("seq")
    me = lax.axis_index("seq")
    window = 2 * REACH + 1
    pair = jnp.stack([keys, values])
    received = {0: pair}
    for heading in (1, -1):
        moving = pair
        for stride in range(1, REACH + 1):
            moving = lax.ppermute(moving, "seq", [(i, (i + heading) % n) for i in range(n)])
            received[-heading * stride] = moving
    both = jnp.stack([received[o] for o in range(-REACH, REACH + 1)])
    both = both.reshape(window, 2, rows, heads, HEAD_DIM).transpose(1, 3, 0, 2, 4)
    q = queries.reshape(rows, heads, HEAD_DIM).transpose(1, 0, 2)[:, None]
    slots, count = listed_slots(kv_tiles, tile_order, me)
    place = (slots - me + REACH) % n
    place = jnp.clip(place, 0, window - 1)
    attended = attention(q, both[0], both[1], place[None], count[None], 0, 1)[0]
    partial = jnp.dot(attended, out_weight, preferred_element_type=jnp.float32).astype(jnp.bfloat16)
    return lax.psum_scatter(partial, "head", scatter_dimension=1, tiled=True)


def exchange_body(
    groups, share, bits, q_ref, k_ref, v_ref, w_ref, q_out, k_out, v_out, w_out,
    local_sem, plane_send, plane_recv, swap_send, swap_recv, w_send, w_recv,
):
    sub = lax.axis_size("seq") // groups
    me = lax.axis_index("seq")
    plane, inner = me // sub, me % sub
    other = 1 - lax.axis_index("head")

    def across(o):
        return {"seq": (plane + o) % groups * sub + inner}

    def swapped(bit):
        return {"seq": plane * sub + inner + bit * (1 - 2 * (inner // bit % 2))}

    partners = [across(o) for o in range(1, groups)] + [swapped(b) for b in bits] + [{"head": other}]
    barrier = pltpu.get_barrier_semaphore()
    for partner in partners:
        pl.semaphore_signal(barrier, inc=1, device_id=partner, device_id_type=MESH)
    pl.semaphore_wait(barrier, len(partners))

    half = w_ref.shape[0] // 2
    columns = w_out.shape[1]
    own_rows = pl.ds(pl.multiple_of(me % 2 * half, half), half)
    w_cross = pltpu.make_async_remote_copy(
        src_ref=w_ref.at[own_rows, pl.ds(pl.multiple_of(other * columns, columns), columns)],
        dst_ref=w_out.at[own_rows],
        send_sem=w_send.at[0],
        recv_sem=w_recv.at[0],
        device_id={"head": other},
        device_id_type=MESH,
    )
    w_cross.start()
    arrays = ((k_ref, k_out), (v_ref, v_out), (q_ref, q_out))

    def cut(ref, to_plane, j):
        start = (to_plane * share + j) * HEAD_DIM
        return ref.at[:, pl.ds(pl.multiple_of(start, HEAD_DIM), HEAD_DIM)]

    local, crossing = {}, {}
    for j in range(share):
        for a, (src, dst) in enumerate(arrays):
            for o in range(1, groups):
                crossing[j, o, a] = pltpu.make_async_remote_copy(
                    src_ref=cut(src, (plane + o) % groups, j),
                    dst_ref=dst.at[j, o],
                    send_sem=plane_send.at[j, o, a],
                    recv_sem=plane_recv.at[j, o, a],
                    device_id=across(o),
                    device_id_type=MESH,
                )
                crossing[j, o, a].start()
            local[j, a] = pltpu.make_async_copy(cut(src, plane, j), dst.at[j, 0], local_sem.at[j, a])
            local[j, a].start()

    swaps = {}

    def start_swap(j, stage):
        held = groups << stage
        for a in range(2):
            out = arrays[a][1]
            swaps[j, stage, a] = pltpu.make_async_remote_copy(
                src_ref=out.at[j, pl.ds(0, held)],
                dst_ref=out.at[j, pl.ds(held, held)],
                send_sem=swap_send.at[j, stage, a],
                recv_sem=swap_recv.at[j, stage, a],
                device_id=swapped(bits[stage]),
                device_id_type=MESH,
            )
            swaps[j, stage, a].start()

    for step in range(share + len(bits)):
        for stage in range(min(step, len(bits)), -1, -1):
            j = step - stage
            if not 0 <= j < share:
                continue
            for a in range(2):
                if stage == 0:
                    local[j, a].wait()
                    for o in range(1, groups):
                        crossing[j, o, a].wait_recv()
                else:
                    swaps[j, stage - 1, a].wait_recv()
            if stage < len(bits):
                start_swap(j, stage)
        if step == share - 1:
            w_cross.wait_recv()
            w_on = pltpu.make_async_remote_copy(
                src_ref=w_out.at[own_rows],
                dst_ref=w_out.at[own_rows],
                send_sem=w_send.at[1],
                recv_sem=w_recv.at[1],
                device_id=swapped(1),
                device_id_type=MESH,
            )
            w_on.start()
    for j in range(share):
        local[j, 2].wait()
        for o in range(1, groups):
            crossing[j, o, 2].wait_recv()
            for a in range(3):
                crossing[j, o, a].wait_send()
        for stage in range(len(bits)):
            for a in range(2):
                swaps[j, stage, a].wait_send()
    w_cross.wait_send()
    w_on.wait()


def exchange(groups, bits, queries, keys, values, out_weight, columns):
    rows, local_width = queries.shape
    share = local_width // HEAD_DIM // groups
    n = lax.axis_size("seq")
    anywhere = pl.BlockSpec(memory_space=pl.ANY)
    kind = jnp.bfloat16
    stages = len(bits)
    return pl.pallas_call(
        functools.partial(exchange_body, groups, share, bits),
        out_shape=(
            jax.ShapeDtypeStruct((share, groups, rows, HEAD_DIM), kind),
            jax.ShapeDtypeStruct((share, n, rows, HEAD_DIM), kind),
            jax.ShapeDtypeStruct((share, n, rows, HEAD_DIM), kind),
            jax.ShapeDtypeStruct((out_weight.shape[0], columns), kind),
        ),
        in_specs=[anywhere] * 4,
        out_specs=(anywhere,) * 4,
        scratch_shapes=[
            pltpu.SemaphoreType.DMA((share, 3)),
            pltpu.SemaphoreType.DMA((share, groups, 3)),
            pltpu.SemaphoreType.DMA((share, groups, 3)),
            pltpu.SemaphoreType.DMA((share, stages, 2)),
            pltpu.SemaphoreType.DMA((share, stages, 2)),
            pltpu.SemaphoreType.DMA((2,)),
            pltpu.SemaphoreType.DMA((2,)),
        ],
        compiler_params=pltpu.CompilerParams(collective_id=0, has_side_effects=True),
    )(queries, keys, values, out_weight)


def project_body(block_ref, own_ref, far_ref, w_own, w_far, out_ref, total):
    step = pl.program_id(0)

    @pl.when(step == 0)
    def _():
        total[...] = jnp.zeros(total.shape, jnp.float32)

    total[...] += jnp.dot(own_ref[0], w_own[...], preferred_element_type=jnp.float32) + jnp.dot(
        far_ref[0], w_far[...], preferred_element_type=jnp.float32
    )

    @pl.when(step == pl.num_programs(0) - 1)
    def _():
        out_ref[...] = total[...].astype(jnp.bfloat16)


def project(blocks, own, far, out_weight, w_far):
    groups, rows, wide = own.shape
    columns = w_far.shape[1]
    term = pl.BlockSpec((1, rows, wide), lambda s, b: (s, 0, 0))
    return pl.pallas_call(
        project_body,
        out_shape=jax.ShapeDtypeStruct((rows, columns), jnp.bfloat16),
        grid_spec=pltpu.PrefetchScalarGridSpec(
            num_scalar_prefetch=1,
            grid=(groups,),
            in_specs=[
                term,
                term,
                pl.BlockSpec((wide, columns), lambda s, b: (b[s], b[groups])),
                pl.BlockSpec((wide, columns), lambda s, b: (b[s], 0)),
            ],
            out_specs=pl.BlockSpec((rows, columns), lambda s, b: (0, 0)),
            scratch_shapes=[pltpu.VMEM((rows, columns), jnp.float32)],
        ),
        compiler_params=pltpu.CompilerParams(vmem_limit_bytes=40 * 1024 * 1024),
    )(blocks, own, far, out_weight, w_far)


def by_heads(groups, queries, keys, values, kv_tiles, tile_order, out_weight):
    n = lax.axis_size("seq")
    sub = n // groups
    me = lax.axis_index("seq")
    plane, inner = me // sub, me % sub
    bits = []
    bit = sub // 2
    while bit:
        bits.append(bit)
        bit //= 2
    mask_place = [sum(1 << i for i, b in enumerate(bits) if mask & b) for mask in range(sub)]
    mask_place = jnp.array(mask_place, jnp.int32)

    places, counts = [], []
    for o in range(groups):
        slots, count = listed_slots(kv_tiles, tile_order, (plane - o) % groups * sub + inner)
        places.append(mask_place[(slots % sub) ^ inner] * groups + (plane - slots // sub) % groups)
        counts.append(count)
    place, count = jnp.stack(places), jnp.stack(counts)

    columns = out_weight.shape[1] // lax.axis_size("head")
    q, k, v, w_far = exchange(groups, bits, queries, keys, values, out_weight, columns)

    def plane_shift(x, by):
        return lax.ppermute(
            x, "seq", [(i, (i // sub + by) % groups * sub + i % sub) for i in range(n)]
        )

    pieces = [None] * groups
    cuts = [(1, groups - 2), (groups - 1, 1), (0, 1)] if groups > 2 else [(1, 1), (0, 1)]
    for first, tiles in cuts:
        attended = attention(q, k, v, place, count, first, tiles)
        for i in range(tiles):
            o = first + i
            pieces[o] = plane_shift(attended[i], -o) if o else attended[i]
    far = [lax.ppermute(piece, "head", [(0, 1), (1, 0)]) for piece in pieces]
    blocks = jnp.stack([(plane + o) % groups for o in range(groups)] + [lax.axis_index("head")])
    return project(blocks.astype(jnp.int32), jnp.stack(pieces), jnp.stack(far), out_weight, w_far)


def per_device(queries, keys, values, kv_tiles, tile_order, out_weight):
    n = lax.axis_size("seq")
    groups = math.gcd(queries.shape[1] // HEAD_DIM, n)
    sub = n // groups
    power_of_two = sub & (sub - 1) == 0
    two_groups = lax.axis_size("head") == 2
    if two_groups and groups > 1 and sub > 1 and power_of_two and n <= 2 * (2 * REACH + 1):
        return by_heads(groups, queries, keys, values, kv_tiles, tile_order, out_weight)
    return by_ring(queries, keys, values, kv_tiles, tile_order, out_weight)


def solution(mesh):
    return jax.shard_map(
        per_device,
        mesh=mesh,
        in_specs=(P("seq", "head"), P("seq", "head"), P("seq", "head"), P(), P(), P("head", None)),
        out_specs=P("seq", "head"),
        check_vma=False,
    )
```

```python
import functools
import math

import jax
import jax.numpy as jnp
from jax import lax
from jax.experimental import pallas as pl
from jax.experimental.pallas import tpu as pltpu
from jax.sharding import PartitionSpec as P

HEAD_DIM = 128
REACH = 6
MESH = pl.DeviceIdType.MESH


def attention_body(
    slot_of_row, place_of_slot, at_ref, tiles_ref, order_ref, q_ref, k_ref, v_ref, out_ref, scores, tops, summed
):
    slots, width = tiles_ref.shape
    at = [at_ref[i] for i in range(at_ref.shape[0])]
    first_tile = order_ref[0]
    own_tile = order_ref[slot_of_row(pl.program_id(0), at)]
    count = 0
    for entry in range(width):
        count += jnp.where(tiles_ref[own_tile, entry] >= 0, 1, 0)

    def place_at(entry):
        slot = lax.rem(tiles_ref[own_tile, entry] - first_tile + slots, slots)
        return place_of_slot(slot, at)

    heads = q_ref.shape[0]
    scale = math.log2(math.e) / math.sqrt(HEAD_DIM)
    tops[...] = jnp.full(tops.shape, -jnp.inf, jnp.float32)
    summed[...] = jnp.zeros(summed.shape, jnp.float32)
    ones = jnp.ones((k_ref.shape[2], HEAD_DIM), jnp.bfloat16)

    def find(entry, carry):
        place = place_at(entry)
        for h in range(heads):
            fresh = lax.dot_general(
                q_ref[h, 0],
                k_ref[h, place],
                (((1,), (1,)), ((), ())),
                preferred_element_type=jnp.float32,
            )
            scores[h, entry] = fresh
            best = tops[h]
            for lane in range(0, fresh.shape[1], HEAD_DIM):
                best = jnp.maximum(best, fresh[:, lane : lane + HEAD_DIM])
            tops[h] = best
        return carry

    lax.fori_loop(0, count, find, 0)
    for h in range(heads):
        top = jnp.max(tops[h], axis=1, keepdims=True) * scale
        tops[h] = jnp.broadcast_to(top, tops.shape[1:])

    def add(entry, carry):
        place = place_at(entry)
        for h in range(heads):
            top = tops[h]
            weights = jnp.concatenate(
                [
                    jnp.exp2(scores[h, entry, :, lane : lane + HEAD_DIM] * scale - top).astype(jnp.bfloat16)
                    for lane in range(0, scores.shape[3], HEAD_DIM)
                ],
                axis=1,
            )
            paired = jnp.concatenate([v_ref[h, place], ones], axis=1)
            summed[h] += jnp.dot(weights, paired, preferred_element_type=jnp.float32)
        return carry

    lax.fori_loop(0, count, add, 0)
    for h in range(heads):
        done = summed[h]
        out_ref[0, :, h * HEAD_DIM : (h + 1) * HEAD_DIM] = (
            done[:, :HEAD_DIM] / done[:, HEAD_DIM:]
        ).astype(jnp.bfloat16)


def attention(q, k, v, at, kv_tiles, tile_order, slot_of_row, place_of_slot, first, tiles):
    heads, _, rows, _ = q.shape
    key_tiles = k.shape[1]
    width = kv_tiles.shape[1]
    units = heads * tiles * min(width, key_tiles)
    key_spec = pl.BlockSpec(
        (heads, key_tiles, rows, HEAD_DIM), lambda t, *_: (0, 0, 0, 0), pipeline_mode=pl.Buffered(1)
    )
    return pl.pallas_call(
        functools.partial(attention_body, slot_of_row, place_of_slot),
        out_shape=jax.ShapeDtypeStruct((tiles, rows, heads * HEAD_DIM), jnp.bfloat16),
        grid_spec=pltpu.PrefetchScalarGridSpec(
            num_scalar_prefetch=3,
            grid=(tiles,),
            in_specs=[
                pl.BlockSpec((heads, 1, rows, HEAD_DIM), lambda t, *_: (0, first + t, 0, 0)),
                key_spec,
                key_spec,
            ],
            out_specs=pl.BlockSpec((1, rows, heads * HEAD_DIM), lambda t, *_: (t, 0, 0)),
            scratch_shapes=[
                pltpu.VMEM((heads, width, rows, rows), jnp.float32),
                pltpu.VMEM((heads, rows, HEAD_DIM), jnp.float32),
                pltpu.VMEM((heads, rows, 2 * HEAD_DIM), jnp.float32),
            ],
        ),
        compiler_params=pltpu.CompilerParams(vmem_limit_bytes=52 * 1024 * 1024),
        cost_estimate=pl.CostEstimate(
            flops=units * rows * rows * HEAD_DIM * 4,
            bytes_accessed=2 * (2 * q.size + k.size + v.size),
            transcendentals=units * rows * rows,
        ),
    )(at, kv_tiles, tile_order, q, k, v)


def by_ring(queries, keys, values, kv_tiles, tile_order, out_weight):
    rows, local_width = queries.shape
    heads = local_width // HEAD_DIM
    n = lax.axis_size("seq")
    me = lax.axis_index("seq")
    window = 2 * REACH + 1
    pair = jnp.stack([keys, values])
    received = {0: pair}
    for heading in (1, -1):
        moving = pair
        for stride in range(1, REACH + 1):
            moving = lax.ppermute(moving, "seq", [(i, (i + heading) % n) for i in range(n)])
            received[-heading * stride] = moving
    both = jnp.stack([received[o] for o in range(-REACH, REACH + 1)])
    both = both.reshape(window, 2, rows, heads, HEAD_DIM).transpose(1, 3, 0, 2, 4)
    q = queries.reshape(rows, heads, HEAD_DIM).transpose(1, 0, 2)[:, None]
    attended = attention(
        q,
        both[0],
        both[1],
        me.reshape(1).astype(jnp.int32),
        kv_tiles,
        tile_order,
        lambda row, at: at[0],
        lambda slot, at: lax.rem(slot - at[0] + REACH + n, n),
        0,
        1,
    )[0]
    partial = jnp.dot(attended, out_weight, preferred_element_type=jnp.float32).astype(jnp.bfloat16)
    return lax.psum_scatter(partial, "head", scatter_dimension=1, tiled=True)


def exchange_body(
    groups, share, bits, q_ref, k_ref, v_ref, w_ref, q_out, k_out, v_out, w_out,
    local_sem, plane_send, plane_recv, swap_send, swap_recv, w_send, w_recv,
):
    sub = lax.axis_size("seq") // groups
    me = lax.axis_index("seq")
    plane, inner = me // sub, me % sub
    other = 1 - lax.axis_index("head")

    def across(o):
        return {"seq": (plane + o) % groups * sub + inner}

    def swapped(bit):
        return {"seq": plane * sub + inner + bit * (1 - 2 * (inner // bit % 2))}

    partners = [across(o) for o in range(1, groups)] + [swapped(b) for b in bits] + [{"head": other}]
    barrier = pltpu.get_barrier_semaphore()
    for partner in partners:
        pl.semaphore_signal(barrier, inc=1, device_id=partner, device_id_type=MESH)
    pl.semaphore_wait(barrier, len(partners))

    half = w_ref.shape[0] // 2
    columns = w_out.shape[1]
    own_rows = pl.ds(pl.multiple_of(me % 2 * half, half), half)
    w_cross = pltpu.make_async_remote_copy(
        src_ref=w_ref.at[own_rows, pl.ds(pl.multiple_of(other * columns, columns), columns)],
        dst_ref=w_out.at[own_rows],
        send_sem=w_send.at[0],
        recv_sem=w_recv.at[0],
        device_id={"head": other},
        device_id_type=MESH,
    )
    w_cross.start()
    arrays = ((k_ref, k_out), (v_ref, v_out), (q_ref, q_out))

    def cut(ref, to_plane, j):
        start = (to_plane * share + j) * HEAD_DIM
        return ref.at[:, pl.ds(pl.multiple_of(start, HEAD_DIM), HEAD_DIM)]

    local, crossing = {}, {}
    for j, a in [(j, a) for j in range(share) for a in (0, 1)] + [(j, 2) for j in range(share)]:
        src, dst = arrays[a]
        for o in range(1, groups):
            crossing[j, o, a] = pltpu.make_async_remote_copy(
                src_ref=cut(src, (plane + o) % groups, j),
                dst_ref=dst.at[j, o],
                send_sem=plane_send.at[j, o, a],
                recv_sem=plane_recv.at[j, o, a],
                device_id=across(o),
                device_id_type=MESH,
            )
            crossing[j, o, a].start()
        local[j, a] = pltpu.make_async_copy(cut(src, plane, j), dst.at[j, 0], local_sem.at[j, a])
        local[j, a].start()

    swaps = {}

    def start_swap(j, stage):
        held = groups << stage
        for a in range(2):
            out = arrays[a][1]
            swaps[j, stage, a] = pltpu.make_async_remote_copy(
                src_ref=out.at[j, pl.ds(0, held)],
                dst_ref=out.at[j, pl.ds(held, held)],
                send_sem=swap_send.at[j, stage, a],
                recv_sem=swap_recv.at[j, stage, a],
                device_id=swapped(bits[stage]),
                device_id_type=MESH,
            )
            swaps[j, stage, a].start()

    for step in range(share + len(bits)):
        for stage in range(min(step, len(bits)), -1, -1):
            j = step - stage
            if not 0 <= j < share:
                continue
            for a in range(2):
                if stage == 0:
                    local[j, a].wait()
                    for o in range(1, groups):
                        crossing[j, o, a].wait_recv()
                else:
                    swaps[j, stage - 1, a].wait_recv()
            if stage < len(bits):
                start_swap(j, stage)
        if step == share - 1:
            w_cross.wait_recv()
            w_on = pltpu.make_async_remote_copy(
                src_ref=w_out.at[own_rows],
                dst_ref=w_out.at[own_rows],
                send_sem=w_send.at[1],
                recv_sem=w_recv.at[1],
                device_id=swapped(1),
                device_id_type=MESH,
            )
            w_on.start()
    for j in range(share):
        local[j, 2].wait()
        for o in range(1, groups):
            crossing[j, o, 2].wait_recv()
            for a in range(3):
                crossing[j, o, a].wait_send()
        for stage in range(len(bits)):
            for a in range(2):
                swaps[j, stage, a].wait_send()
    w_cross.wait_send()
    w_on.wait()


def exchange(groups, bits, queries, keys, values, out_weight, columns):
    rows, local_width = queries.shape
    share = local_width // HEAD_DIM // groups
    n = lax.axis_size("seq")
    anywhere = pl.BlockSpec(memory_space=pl.ANY)
    kind = jnp.bfloat16
    stages = len(bits)
    return pl.pallas_call(
        functools.partial(exchange_body, groups, share, bits),
        out_shape=(
            jax.ShapeDtypeStruct((share, groups, rows, HEAD_DIM), kind),
            jax.ShapeDtypeStruct((share, n, rows, HEAD_DIM), kind),
            jax.ShapeDtypeStruct((share, n, rows, HEAD_DIM), kind),
            jax.ShapeDtypeStruct((out_weight.shape[0], columns), kind),
        ),
        in_specs=[anywhere] * 4,
        out_specs=(anywhere,) * 4,
        scratch_shapes=[
            pltpu.SemaphoreType.DMA((share, 3)),
            pltpu.SemaphoreType.DMA((share, groups, 3)),
            pltpu.SemaphoreType.DMA((share, groups, 3)),
            pltpu.SemaphoreType.DMA((share, stages, 2)),
            pltpu.SemaphoreType.DMA((share, stages, 2)),
            pltpu.SemaphoreType.DMA((2,)),
            pltpu.SemaphoreType.DMA((2,)),
        ],
        compiler_params=pltpu.CompilerParams(collective_id=0, has_side_effects=True),
    )(queries, keys, values, out_weight)


def project_body(first, at_ref, term_ref, weight_ref, *refs):
    base_ref, out_ref, total = (None, *refs) if first else refs
    step = pl.program_id(0)

    @pl.when(step == 0)
    def _():
        total[...] = jnp.zeros(total.shape, jnp.float32) if first else base_ref[...]

    total[...] += jnp.dot(term_ref[0], weight_ref[...], preferred_element_type=jnp.float32)

    @pl.when(step == pl.num_programs(0) - 1)
    def _():
        out_ref[...] = total[...].astype(out_ref.dtype)


def project(at, terms, weight, column_entry, base):
    groups, rows, wide = terms.shape
    first = base is None
    columns = weight.shape[1] // (lax.axis_size("head") if first else 1)
    whole = pl.BlockSpec((rows, columns), lambda s, at: (0, 0))
    return pl.pallas_call(
        functools.partial(project_body, first),
        out_shape=jax.ShapeDtypeStruct((rows, columns), jnp.float32 if first else jnp.bfloat16),
        grid_spec=pltpu.PrefetchScalarGridSpec(
            num_scalar_prefetch=1,
            grid=(groups,),
            in_specs=[
                pl.BlockSpec((1, rows, wide), lambda s, at: (s, 0, 0)),
                pl.BlockSpec((wide, columns), lambda s, at: (at[2 + s], at[column_entry] if first else 0)),
            ]
            + ([] if first else [whole]),
            out_specs=whole,
            scratch_shapes=[pltpu.VMEM((rows, columns), jnp.float32)],
        ),
        compiler_params=pltpu.CompilerParams(vmem_limit_bytes=40 * 1024 * 1024),
        cost_estimate=pl.CostEstimate(
            flops=2 * groups * rows * wide * columns,
            bytes_accessed=2 * groups * wide * columns + 6 * rows * columns,
            transcendentals=0,
        ),
    )(at, terms, weight, *([] if first else [base]))


def by_heads(groups, queries, keys, values, kv_tiles, tile_order, out_weight):
    n = lax.axis_size("seq")
    sub = n // groups
    me = lax.axis_index("seq")
    plane, inner = me // sub, me % sub
    bits = []
    bit = sub // 2
    while bit:
        bits.append(bit)
        bit //= 2
    head = lax.axis_index("head")
    at = jnp.stack([plane, inner] + [(plane + o) % groups for o in range(groups)] + [head])
    at = at.astype(jnp.int32)

    def slot_of_row(first, row, at):
        return lax.rem(at[0] - first - row + groups, groups) * sub + at[1]

    def place_of_slot(slot, at):
        from_plane = lax.div(slot, sub)
        place = lax.rem(at[0] - from_plane + groups, groups)
        for stage, bit in enumerate(bits):
            differs = lax.rem(lax.div(slot, bit) + lax.div(at[1], bit), 2)
            place += differs * (groups << stage)
        return place

    columns = out_weight.shape[1] // lax.axis_size("head")
    q, k, v, w_far = exchange(groups, bits, queries, keys, values, out_weight, columns)

    def plane_shift(x, by):
        return lax.ppermute(
            x, "seq", [(i, (i // sub + by) % groups * sub + i % sub) for i in range(n)]
        )

    pieces, far = [None] * groups, [None] * groups

    def attend(first, tiles, q):
        rows_of = functools.partial(slot_of_row, first)
        found = attention(q, k, v, at, kv_tiles, tile_order, rows_of, place_of_slot, first, tiles)
        for i in range(tiles):
            o = first + i
            pieces[o] = plane_shift(found[i], -o) if o else found[i]

    def to_far(which):
        for o in which:
            far[o] = lax.ppermute(pieces[o], "head", [(0, 1), (1, 0)])

    early = list(range(1, groups - 1))
    if early:
        attend(1, len(early), q)
        attend(groups - 1, 1, q)
        held, q = lax.optimization_barrier(([pieces[o] for o in early], q))
        for o, piece in zip(early, held):
            pieces[o] = piece
        to_far(early)
    else:
        attend(groups - 1, 1, q)
    attend(0, 1, q)
    held, pieces[0] = lax.optimization_barrier(([far[o] for o in early], pieces[0]))
    for o, piece in zip(early, held):
        far[o] = piece
    to_far([0, groups - 1])
    half_way = project(at, jnp.stack(pieces), out_weight, 2 + groups, None)
    return project(at, jnp.stack(far), w_far, None, half_way)


def per_device(queries, keys, values, kv_tiles, tile_order, out_weight):
    n = lax.axis_size("seq")
    groups = math.gcd(queries.shape[1] // HEAD_DIM, n)
    sub = n // groups
    power_of_two = sub & (sub - 1) == 0
    two_groups = lax.axis_size("head") == 2
    if two_groups and groups > 1 and sub > 1 and power_of_two and n <= 2 * (2 * REACH + 1):
        return by_heads(groups, queries, keys, values, kv_tiles, tile_order, out_weight)
    return by_ring(queries, keys, values, kv_tiles, tile_order, out_weight)


def solution(mesh):
    return jax.shard_map(
        per_device,
        mesh=mesh,
        in_specs=(P("seq", "head"), P("seq", "head"), P("seq", "head"), P(), P(), P("head", None)),
        out_specs=P("seq", "head"),
        check_vma=False,
    )
```

```python
import functools
import math

import jax
import jax.numpy as jnp
from jax import lax
from jax.experimental import pallas as pl
from jax.experimental.pallas import tpu as pltpu
from jax.sharding import PartitionSpec as P

HEAD_DIM = 128
REACH = 6
MESH = pl.DeviceIdType.MESH


def attention_body(
    slot_of_row, place_of_slot, at_ref, tiles_ref, order_ref, q_ref, k_ref, v_ref, out_ref, scores, tops, summed
):
    slots, width = tiles_ref.shape
    at = [at_ref[i] for i in range(at_ref.shape[0])]
    first_tile = order_ref[0]
    own_tile = order_ref[slot_of_row(pl.program_id(0), at)]
    count = 0
    for entry in range(width):
        count += jnp.where(tiles_ref[own_tile, entry] >= 0, 1, 0)

    def place_at(entry):
        slot = lax.rem(tiles_ref[own_tile, entry] - first_tile + slots, slots)
        return place_of_slot(slot, at)

    heads = q_ref.shape[0]
    scale = math.log2(math.e) / math.sqrt(HEAD_DIM)
    tops[...] = jnp.full(tops.shape, -jnp.inf, jnp.float32)
    summed[...] = jnp.zeros(summed.shape, jnp.float32)
    ones = jnp.ones((k_ref.shape[2], HEAD_DIM), jnp.bfloat16)

    def find(entry, carry):
        place = place_at(entry)
        for h in range(heads):
            fresh = lax.dot_general(
                q_ref[h, 0],
                k_ref[h, place],
                (((1,), (1,)), ((), ())),
                preferred_element_type=jnp.float32,
            )
            scores[h, entry] = fresh
            best = tops[h]
            for lane in range(0, fresh.shape[1], HEAD_DIM):
                best = jnp.maximum(best, fresh[:, lane : lane + HEAD_DIM])
            tops[h] = best
        return carry

    lax.fori_loop(0, count, find, 0)
    for h in range(heads):
        top = jnp.max(tops[h], axis=1, keepdims=True) * scale
        tops[h] = jnp.broadcast_to(top, tops.shape[1:])

    def add(entry, carry):
        place = place_at(entry)
        for h in range(heads):
            top = tops[h]
            weights = jnp.concatenate(
                [
                    jnp.exp2(scores[h, entry, :, lane : lane + HEAD_DIM] * scale - top).astype(jnp.bfloat16)
                    for lane in range(0, scores.shape[3], HEAD_DIM)
                ],
                axis=1,
            )
            paired = jnp.concatenate([v_ref[h, place], ones], axis=1)
            summed[h] += jnp.dot(weights, paired, preferred_element_type=jnp.float32)
        return carry

    lax.fori_loop(0, count, add, 0)
    for h in range(heads):
        done = summed[h]
        out_ref[0, :, h * HEAD_DIM : (h + 1) * HEAD_DIM] = (
            done[:, :HEAD_DIM] / done[:, HEAD_DIM:]
        ).astype(jnp.bfloat16)


def attention(q, k, v, at, kv_tiles, tile_order, slot_of_row, place_of_slot, tiles):
    heads, _, rows, _ = q.shape
    key_tiles = k.shape[1]
    width = kv_tiles.shape[1]
    units = heads * tiles * min(width, key_tiles)
    key_spec = pl.BlockSpec(
        (heads, key_tiles, rows, HEAD_DIM), lambda t, *_: (0, 0, 0, 0), pipeline_mode=pl.Buffered(1)
    )
    return pl.pallas_call(
        functools.partial(attention_body, slot_of_row, place_of_slot),
        out_shape=jax.ShapeDtypeStruct((tiles, rows, heads * HEAD_DIM), jnp.bfloat16),
        grid_spec=pltpu.PrefetchScalarGridSpec(
            num_scalar_prefetch=3,
            grid=(tiles,),
            in_specs=[
                pl.BlockSpec((heads, 1, rows, HEAD_DIM), lambda t, *_: (0, t, 0, 0)),
                key_spec,
                key_spec,
            ],
            out_specs=pl.BlockSpec((1, rows, heads * HEAD_DIM), lambda t, *_: (t, 0, 0)),
            scratch_shapes=[
                pltpu.VMEM((heads, width, rows, rows), jnp.float32),
                pltpu.VMEM((heads, rows, HEAD_DIM), jnp.float32),
                pltpu.VMEM((heads, rows, 2 * HEAD_DIM), jnp.float32),
            ],
        ),
        compiler_params=pltpu.CompilerParams(vmem_limit_bytes=52 * 1024 * 1024),
        cost_estimate=pl.CostEstimate(
            flops=units * rows * rows * HEAD_DIM * 4,
            bytes_accessed=2 * (2 * q.size + k.size + v.size),
            transcendentals=units * rows * rows,
        ),
    )(at, kv_tiles, tile_order, q, k, v)


def by_ring(queries, keys, values, kv_tiles, tile_order, out_weight):
    rows, local_width = queries.shape
    heads = local_width // HEAD_DIM
    n = lax.axis_size("seq")
    me = lax.axis_index("seq")
    window = 2 * REACH + 1
    pair = jnp.stack([keys, values])
    received = {0: pair}
    for heading in (1, -1):
        moving = pair
        for stride in range(1, REACH + 1):
            moving = lax.ppermute(moving, "seq", [(i, (i + heading) % n) for i in range(n)])
            received[-heading * stride] = moving
    both = jnp.stack([received[o] for o in range(-REACH, REACH + 1)])
    both = both.reshape(window, 2, rows, heads, HEAD_DIM).transpose(1, 3, 0, 2, 4)
    q = queries.reshape(rows, heads, HEAD_DIM).transpose(1, 0, 2)[:, None]
    attended = attention(
        q,
        both[0],
        both[1],
        me.reshape(1).astype(jnp.int32),
        kv_tiles,
        tile_order,
        lambda row, at: at[0],
        lambda slot, at: lax.rem(slot - at[0] + REACH + n, n),
        1,
    )[0]
    partial = jnp.dot(attended, out_weight, preferred_element_type=jnp.float32).astype(jnp.bfloat16)
    return lax.psum_scatter(partial, "head", scatter_dimension=1, tiled=True)


def exchange_body(
    groups, share, bits, q_ref, k_ref, v_ref, w_ref, q_out, k_out, v_out, w_out,
    local_sem, plane_send, plane_recv, swap_send, swap_recv, w_send, w_recv,
):
    sub = lax.axis_size("seq") // groups
    me = lax.axis_index("seq")
    plane, inner = me // sub, me % sub
    other = 1 - lax.axis_index("head")

    def across(o):
        return {"seq": (plane + o) % groups * sub + inner}

    def swapped(bit):
        return {"seq": plane * sub + inner + bit * (1 - 2 * (inner // bit % 2))}

    partners = [across(o) for o in range(1, groups)] + [swapped(b) for b in bits] + [{"head": other}]
    barrier = pltpu.get_barrier_semaphore()
    for partner in partners:
        pl.semaphore_signal(barrier, inc=1, device_id=partner, device_id_type=MESH)
    pl.semaphore_wait(barrier, len(partners))

    half = w_ref.shape[0] // 2
    columns = w_out.shape[1]
    own_rows = pl.ds(pl.multiple_of(me % 2 * half, half), half)
    w_cross = pltpu.make_async_remote_copy(
        src_ref=w_ref.at[own_rows, pl.ds(pl.multiple_of(other * columns, columns), columns)],
        dst_ref=w_out.at[own_rows],
        send_sem=w_send.at[0],
        recv_sem=w_recv.at[0],
        device_id={"head": other},
        device_id_type=MESH,
    )
    w_cross.start()
    arrays = ((k_ref, k_out), (v_ref, v_out), (q_ref, q_out))

    def cut(ref, to_plane, j):
        start = (to_plane * share + j) * HEAD_DIM
        return ref.at[:, pl.ds(pl.multiple_of(start, HEAD_DIM), HEAD_DIM)]

    local, crossing = {}, {}
    for j, a in [(j, a) for j in range(share) for a in (0, 1)] + [(j, 2) for j in range(share)]:
        src, dst = arrays[a]
        for o in range(1, groups):
            crossing[j, o, a] = pltpu.make_async_remote_copy(
                src_ref=cut(src, (plane + o) % groups, j),
                dst_ref=dst.at[j, o],
                send_sem=plane_send.at[j, o, a],
                recv_sem=plane_recv.at[j, o, a],
                device_id=across(o),
                device_id_type=MESH,
            )
            crossing[j, o, a].start()
        local[j, a] = pltpu.make_async_copy(cut(src, plane, j), dst.at[j, 0], local_sem.at[j, a])
        local[j, a].start()

    swaps = {}

    def start_swap(j, stage):
        held = groups << stage
        for a in range(2):
            out = arrays[a][1]
            swaps[j, stage, a] = pltpu.make_async_remote_copy(
                src_ref=out.at[j, pl.ds(0, held)],
                dst_ref=out.at[j, pl.ds(held, held)],
                send_sem=swap_send.at[j, stage, a],
                recv_sem=swap_recv.at[j, stage, a],
                device_id=swapped(bits[stage]),
                device_id_type=MESH,
            )
            swaps[j, stage, a].start()

    for step in range(share + len(bits)):
        for stage in range(min(step, len(bits)), -1, -1):
            j = step - stage
            if not 0 <= j < share:
                continue
            for a in range(2):
                if stage == 0:
                    local[j, a].wait()
                    for o in range(1, groups):
                        crossing[j, o, a].wait_recv()
                else:
                    swaps[j, stage - 1, a].wait_recv()
            if stage < len(bits):
                start_swap(j, stage)
        if step == share - 1:
            w_cross.wait_recv()
            w_on = pltpu.make_async_remote_copy(
                src_ref=w_out.at[own_rows],
                dst_ref=w_out.at[own_rows],
                send_sem=w_send.at[1],
                recv_sem=w_recv.at[1],
                device_id=swapped(1),
                device_id_type=MESH,
            )
            w_on.start()
    for j in range(share):
        local[j, 2].wait()
        for o in range(1, groups):
            crossing[j, o, 2].wait_recv()
            for a in range(3):
                crossing[j, o, a].wait_send()
        for stage in range(len(bits)):
            for a in range(2):
                swaps[j, stage, a].wait_send()
    w_cross.wait_send()
    w_on.wait()


def exchange(groups, bits, queries, keys, values, out_weight, columns):
    rows, local_width = queries.shape
    share = local_width // HEAD_DIM // groups
    n = lax.axis_size("seq")
    anywhere = pl.BlockSpec(memory_space=pl.ANY)
    kind = jnp.bfloat16
    stages = len(bits)
    return pl.pallas_call(
        functools.partial(exchange_body, groups, share, bits),
        out_shape=(
            jax.ShapeDtypeStruct((share, groups, rows, HEAD_DIM), kind),
            jax.ShapeDtypeStruct((share, n, rows, HEAD_DIM), kind),
            jax.ShapeDtypeStruct((share, n, rows, HEAD_DIM), kind),
            jax.ShapeDtypeStruct((out_weight.shape[0], columns), kind),
        ),
        in_specs=[anywhere] * 4,
        out_specs=(anywhere,) * 4,
        scratch_shapes=[
            pltpu.SemaphoreType.DMA((share, 3)),
            pltpu.SemaphoreType.DMA((share, groups, 3)),
            pltpu.SemaphoreType.DMA((share, groups, 3)),
            pltpu.SemaphoreType.DMA((share, stages, 2)),
            pltpu.SemaphoreType.DMA((share, stages, 2)),
            pltpu.SemaphoreType.DMA((2,)),
            pltpu.SemaphoreType.DMA((2,)),
        ],
        compiler_params=pltpu.CompilerParams(collective_id=0, has_side_effects=True),
    )(queries, keys, values, out_weight)


def deliver_body(
    groups, att_ref, w_ref, w_far_ref, out_ref, home, far, w_own_here, w_far_here, total,
    w_sem, home_send, home_recv, far_send, far_recv,
):
    sub = lax.axis_size("seq") // groups
    me = lax.axis_index("seq")
    plane, inner = me // sub, me % sub
    head = lax.axis_index("head")
    other = {"head": 1 - head}
    rows, wide = att_ref.shape[1:]
    columns = out_ref.shape[1]

    def across(o):
        return {"seq": (plane + o) % groups * sub + inner}

    own_columns = pl.ds(pl.multiple_of(head * columns, columns), columns)
    fetch_own = pltpu.make_async_copy(w_ref.at[:, own_columns], w_own_here, w_sem.at[0])
    fetch_far = pltpu.make_async_copy(w_far_ref, w_far_here, w_sem.at[1])
    fetch_own.start()
    fetch_far.start()

    barrier = pltpu.get_barrier_semaphore()
    for partner in [across(o) for o in range(1, groups)] + [other]:
        pl.semaphore_signal(barrier, inc=1, device_id=partner, device_id_type=MESH)
    pl.semaphore_wait(barrier, groups)

    def on(src, o):
        copy = pltpu.make_async_remote_copy(
            src_ref=src.at[o],
            dst_ref=far.at[o],
            send_sem=far_send.at[o],
            recv_sem=far_recv.at[o],
            device_id=other,
            device_id_type=MESH,
        )
        copy.start()
        return copy

    going = {}
    for o in range(1, groups):
        going[o] = pltpu.make_async_remote_copy(
            src_ref=att_ref.at[o],
            dst_ref=home.at[o],
            send_sem=home_send.at[o],
            recv_sem=home_recv.at[o],
            device_id=across(groups - o),
            device_id_type=MESH,
        )
        going[o].start()
    crossing = {0: on(att_ref, 0)}

    tile = math.gcd(columns, 3 * HEAD_DIM)

    def multiply(src, o, weight, first):
        block = pl.ds(pl.multiple_of((plane + o) % groups * wide, wide), wide)

        def some_columns(i, carry):
            here = pl.ds(pl.multiple_of(i * tile, tile), tile)
            term = jnp.dot(src[o], weight[block, here], preferred_element_type=jnp.float32)
            total[:, here] = term if first else total[:, here] + term
            return carry

        lax.fori_loop(0, columns // tile, some_columns, 0)

    fetch_own.wait()
    multiply(att_ref, 0, w_own_here, True)
    for o in range(1, groups):
        going[o].wait_recv()
        crossing[o] = on(home, o)
        multiply(home, o, w_own_here, False)
    fetch_far.wait()
    for o in range(groups):
        crossing[o].wait_recv()
        multiply(far, o, w_far_here, False)
    out_ref[...] = total[...].astype(jnp.bfloat16)
    for o in range(1, groups):
        going[o].wait_send()
    for o in range(groups):
        crossing[o].wait_send()


def deliver(attended, out_weight, w_far):
    groups, rows, wide = attended.shape
    depth, columns = w_far.shape
    anywhere = pl.BlockSpec(memory_space=pl.ANY)
    here = pl.BlockSpec(memory_space=pltpu.VMEM)
    kind = jnp.bfloat16
    return pl.pallas_call(
        functools.partial(deliver_body, groups),
        out_shape=jax.ShapeDtypeStruct((rows, columns), kind),
        in_specs=[here, anywhere, anywhere],
        out_specs=here,
        scratch_shapes=[
            pltpu.VMEM((groups, rows, wide), kind),
            pltpu.VMEM((groups, rows, wide), kind),
            pltpu.VMEM((depth, columns), kind),
            pltpu.VMEM((depth, columns), kind),
            pltpu.VMEM((rows, columns), jnp.float32),
            pltpu.SemaphoreType.DMA((2,)),
            pltpu.SemaphoreType.DMA((groups,)),
            pltpu.SemaphoreType.DMA((groups,)),
            pltpu.SemaphoreType.DMA((groups,)),
            pltpu.SemaphoreType.DMA((groups,)),
        ],
        compiler_params=pltpu.CompilerParams(
            collective_id=1, has_side_effects=True, vmem_limit_bytes=40 * 1024 * 1024
        ),
    )(attended, out_weight, w_far)


def by_heads(groups, queries, keys, values, kv_tiles, tile_order, out_weight):
    n = lax.axis_size("seq")
    sub = n // groups
    me = lax.axis_index("seq")
    plane, inner = me // sub, me % sub
    bits = []
    bit = sub // 2
    while bit:
        bits.append(bit)
        bit //= 2
    at = jnp.stack([plane, inner]).astype(jnp.int32)

    def slot_of_row(row, at):
        return lax.rem(at[0] - row + groups, groups) * sub + at[1]

    def place_of_slot(slot, at):
        from_plane = lax.div(slot, sub)
        place = lax.rem(at[0] - from_plane + groups, groups)
        for stage, bit in enumerate(bits):
            differs = lax.rem(lax.div(slot, bit) + lax.div(at[1], bit), 2)
            place += differs * (groups << stage)
        return place

    columns = out_weight.shape[1] // lax.axis_size("head")
    q, k, v, w_far = exchange(groups, bits, queries, keys, values, out_weight, columns)

    attended = attention(q, k, v, at, kv_tiles, tile_order, slot_of_row, place_of_slot, groups)
    return deliver(attended, out_weight, w_far)


def per_device(queries, keys, values, kv_tiles, tile_order, out_weight):
    n = lax.axis_size("seq")
    groups = math.gcd(queries.shape[1] // HEAD_DIM, n)
    sub = n // groups
    power_of_two = sub & (sub - 1) == 0
    two_groups = lax.axis_size("head") == 2
    if two_groups and groups > 1 and sub > 1 and power_of_two and n <= 2 * (2 * REACH + 1):
        return by_heads(groups, queries, keys, values, kv_tiles, tile_order, out_weight)
    return by_ring(queries, keys, values, kv_tiles, tile_order, out_weight)


def solution(mesh):
    return jax.shard_map(
        per_device,
        mesh=mesh,
        in_specs=(P("seq", "head"), P("seq", "head"), P("seq", "head"), P(), P(), P("head", None)),
        out_specs=P("seq", "head"),
        check_vma=False,
    )
```

```python
import functools
import math

import jax
import jax.numpy as jnp
from jax import lax
from jax.experimental import pallas as pl
from jax.experimental.pallas import tpu as pltpu
from jax.sharding import PartitionSpec as P

HEAD_DIM = 128
REACH = 6
MESH = pl.DeviceIdType.MESH


def attention_body(
    slot_of_row, place_of_slot, at_ref, tiles_ref, order_ref, q_ref, k_ref, v_ref, out_ref, scores, tops, summed
):
    slots, width = tiles_ref.shape
    at = [at_ref[i] for i in range(at_ref.shape[0])]
    first_tile = order_ref[0]
    own_tile = order_ref[slot_of_row(pl.program_id(0), at)]
    count = 0
    for entry in range(width):
        count += jnp.where(tiles_ref[own_tile, entry] >= 0, 1, 0)

    def place_at(entry):
        slot = lax.rem(tiles_ref[own_tile, entry] - first_tile + slots, slots)
        return place_of_slot(slot, at)

    heads = q_ref.shape[0]
    scale = math.log2(math.e) / math.sqrt(HEAD_DIM)
    tops[...] = jnp.full(tops.shape, -jnp.inf, jnp.float32)
    summed[...] = jnp.zeros(summed.shape, jnp.float32)
    ones = jnp.ones((k_ref.shape[2], HEAD_DIM), jnp.bfloat16)

    def find(entry, carry):
        place = place_at(entry)
        for h in range(heads):
            fresh = lax.dot_general(
                q_ref[h, 0],
                k_ref[h, place],
                (((1,), (1,)), ((), ())),
                preferred_element_type=jnp.float32,
            )
            scores[h, entry] = fresh
            best = tops[h]
            for lane in range(0, fresh.shape[1], HEAD_DIM):
                best = jnp.maximum(best, fresh[:, lane : lane + HEAD_DIM])
            tops[h] = best
        return carry

    lax.fori_loop(0, count, find, 0)
    for h in range(heads):
        top = jnp.max(tops[h], axis=1, keepdims=True) * scale
        tops[h] = jnp.broadcast_to(top, tops.shape[1:])

    def add(entry, carry):
        place = place_at(entry)
        for h in range(heads):
            top = tops[h]
            weights = jnp.concatenate(
                [
                    jnp.exp2(scores[h, entry, :, lane : lane + HEAD_DIM] * scale - top).astype(jnp.bfloat16)
                    for lane in range(0, scores.shape[3], HEAD_DIM)
                ],
                axis=1,
            )
            paired = jnp.concatenate([v_ref[h, place], ones], axis=1)
            summed[h] += jnp.dot(weights, paired, preferred_element_type=jnp.float32)
        return carry

    lax.fori_loop(0, count, add, 0)
    for h in range(heads):
        done = summed[h]
        out_ref[0, :, h * HEAD_DIM : (h + 1) * HEAD_DIM] = (
            done[:, :HEAD_DIM] / done[:, HEAD_DIM:]
        ).astype(jnp.bfloat16)


def attention(q, k, v, at, kv_tiles, tile_order, slot_of_row, place_of_slot, first, tiles):
    heads, _, rows, _ = q.shape
    key_tiles = k.shape[1]
    width = kv_tiles.shape[1]
    units = heads * tiles * min(width, key_tiles)
    key_spec = pl.BlockSpec(
        (heads, key_tiles, rows, HEAD_DIM), lambda t, *_: (0, 0, 0, 0), pipeline_mode=pl.Buffered(1)
    )
    return pl.pallas_call(
        functools.partial(attention_body, slot_of_row, place_of_slot),
        out_shape=jax.ShapeDtypeStruct((tiles, rows, heads * HEAD_DIM), jnp.bfloat16),
        grid_spec=pltpu.PrefetchScalarGridSpec(
            num_scalar_prefetch=3,
            grid=(tiles,),
            in_specs=[
                pl.BlockSpec((heads, 1, rows, HEAD_DIM), lambda t, *_: (0, first + 2 * t, 0, 0)),
                key_spec,
                key_spec,
            ],
            out_specs=pl.BlockSpec((1, rows, heads * HEAD_DIM), lambda t, *_: (t, 0, 0)),
            scratch_shapes=[
                pltpu.VMEM((heads, width, rows, rows), jnp.float32),
                pltpu.VMEM((heads, rows, HEAD_DIM), jnp.float32),
                pltpu.VMEM((heads, rows, 2 * HEAD_DIM), jnp.float32),
            ],
        ),
        compiler_params=pltpu.CompilerParams(vmem_limit_bytes=52 * 1024 * 1024),
        cost_estimate=pl.CostEstimate(
            flops=units * rows * rows * HEAD_DIM * 4,
            bytes_accessed=2 * (2 * q.size + k.size + v.size),
            transcendentals=units * rows * rows,
        ),
    )(at, kv_tiles, tile_order, q, k, v)


def by_ring(queries, keys, values, kv_tiles, tile_order, out_weight):
    rows, local_width = queries.shape
    heads = local_width // HEAD_DIM
    n = lax.axis_size("seq")
    me = lax.axis_index("seq")
    window = 2 * REACH + 1
    pair = jnp.stack([keys, values])
    received = {0: pair}
    for heading in (1, -1):
        moving = pair
        for stride in range(1, REACH + 1):
            moving = lax.ppermute(moving, "seq", [(i, (i + heading) % n) for i in range(n)])
            received[-heading * stride] = moving
    both = jnp.stack([received[o] for o in range(-REACH, REACH + 1)])
    both = both.reshape(window, 2, rows, heads, HEAD_DIM).transpose(1, 3, 0, 2, 4)
    q = queries.reshape(rows, heads, HEAD_DIM).transpose(1, 0, 2)[:, None]
    attended = attention(
        q,
        both[0],
        both[1],
        me.reshape(1).astype(jnp.int32),
        kv_tiles,
        tile_order,
        lambda row, at: at[0],
        lambda slot, at: lax.rem(slot - at[0] + REACH + n, n),
        0,
        1,
    )[0]
    partial = jnp.dot(attended, out_weight, preferred_element_type=jnp.float32).astype(jnp.bfloat16)
    return lax.psum_scatter(partial, "head", scatter_dimension=1, tiled=True)


def exchange_body(
    groups, share, bits, q_ref, k_ref, v_ref, w_ref, q_out, k_out, v_out, w_out,
    local_sem, plane_send, plane_recv, swap_send, swap_recv, w_send, w_recv,
):
    sub = lax.axis_size("seq") // groups
    me = lax.axis_index("seq")
    plane, inner = me // sub, me % sub
    other = 1 - lax.axis_index("head")

    def across(o):
        return {"seq": (plane + o) % groups * sub + inner}

    def swapped(bit):
        return {"seq": plane * sub + inner + bit * (1 - 2 * (inner // bit % 2))}

    partners = [across(o) for o in range(1, groups)] + [swapped(b) for b in bits] + [{"head": other}]
    barrier = pltpu.get_barrier_semaphore()
    for partner in partners:
        pl.semaphore_signal(barrier, inc=1, device_id=partner, device_id_type=MESH)
    pl.semaphore_wait(barrier, len(partners))

    half = w_ref.shape[0] // 2
    columns = w_out.shape[1]
    own_rows = pl.ds(pl.multiple_of(me % 2 * half, half), half)
    w_cross = pltpu.make_async_remote_copy(
        src_ref=w_ref.at[own_rows, pl.ds(pl.multiple_of(other * columns, columns), columns)],
        dst_ref=w_out.at[own_rows],
        send_sem=w_send.at[0],
        recv_sem=w_recv.at[0],
        device_id={"head": other},
        device_id_type=MESH,
    )
    w_cross.start()
    arrays = ((k_ref, k_out), (v_ref, v_out), (q_ref, q_out))

    def cut(ref, to_plane, j):
        start = (to_plane * share + j) * HEAD_DIM
        return ref.at[:, pl.ds(pl.multiple_of(start, HEAD_DIM), HEAD_DIM)]

    local, crossing = {}, {}
    for j, a in [(j, a) for j in range(share) for a in (0, 1)] + [(j, 2) for j in range(share)]:
        src, dst = arrays[a]
        for o in range(1, groups):
            crossing[j, o, a] = pltpu.make_async_remote_copy(
                src_ref=cut(src, (plane + o) % groups, j),
                dst_ref=dst.at[j, o],
                send_sem=plane_send.at[j, o, a],
                recv_sem=plane_recv.at[j, o, a],
                device_id=across(o),
                device_id_type=MESH,
            )
            crossing[j, o, a].start()
        local[j, a] = pltpu.make_async_copy(cut(src, plane, j), dst.at[j, 0], local_sem.at[j, a])
        local[j, a].start()

    swaps = {}

    def start_swap(j, stage):
        held = groups << stage
        for a in range(2):
            out = arrays[a][1]
            swaps[j, stage, a] = pltpu.make_async_remote_copy(
                src_ref=out.at[j, pl.ds(0, held)],
                dst_ref=out.at[j, pl.ds(held, held)],
                send_sem=swap_send.at[j, stage, a],
                recv_sem=swap_recv.at[j, stage, a],
                device_id=swapped(bits[stage]),
                device_id_type=MESH,
            )
            swaps[j, stage, a].start()

    for step in range(share + len(bits)):
        for stage in range(min(step, len(bits)), -1, -1):
            j = step - stage
            if not 0 <= j < share:
                continue
            for a in range(2):
                if stage == 0:
                    local[j, a].wait()
                    for o in range(1, groups):
                        crossing[j, o, a].wait_recv()
                else:
                    swaps[j, stage - 1, a].wait_recv()
            if stage < len(bits):
                start_swap(j, stage)
        if step == share - 1:
            w_cross.wait_recv()
            w_on = pltpu.make_async_remote_copy(
                src_ref=w_out.at[own_rows],
                dst_ref=w_out.at[own_rows],
                send_sem=w_send.at[1],
                recv_sem=w_recv.at[1],
                device_id=swapped(1),
                device_id_type=MESH,
            )
            w_on.start()
    for j in range(share):
        local[j, 2].wait()
        for o in range(1, groups):
            crossing[j, o, 2].wait_recv()
            for a in range(3):
                crossing[j, o, a].wait_send()
        for stage in range(len(bits)):
            for a in range(2):
                swaps[j, stage, a].wait_send()
    w_cross.wait_send()
    w_on.wait()


def exchange(groups, bits, queries, keys, values, out_weight, columns):
    rows, local_width = queries.shape
    share = local_width // HEAD_DIM // groups
    n = lax.axis_size("seq")
    anywhere = pl.BlockSpec(memory_space=pl.ANY)
    kind = jnp.bfloat16
    stages = len(bits)
    return pl.pallas_call(
        functools.partial(exchange_body, groups, share, bits),
        out_shape=(
            jax.ShapeDtypeStruct((share, groups, rows, HEAD_DIM), kind),
            jax.ShapeDtypeStruct((share, n, rows, HEAD_DIM), kind),
            jax.ShapeDtypeStruct((share, n, rows, HEAD_DIM), kind),
            jax.ShapeDtypeStruct((out_weight.shape[0], columns), kind),
        ),
        in_specs=[anywhere] * 4,
        out_specs=(anywhere,) * 4,
        scratch_shapes=[
            pltpu.SemaphoreType.DMA((share, 3)),
            pltpu.SemaphoreType.DMA((share, groups, 3)),
            pltpu.SemaphoreType.DMA((share, groups, 3)),
            pltpu.SemaphoreType.DMA((share, stages, 2)),
            pltpu.SemaphoreType.DMA((share, stages, 2)),
            pltpu.SemaphoreType.DMA((2,)),
            pltpu.SemaphoreType.DMA((2,)),
        ],
        compiler_params=pltpu.CompilerParams(collective_id=0, has_side_effects=True),
    )(queries, keys, values, out_weight)


def project_body(first, at_ref, term_ref, weight_ref, *refs):
    base_ref, out_ref, total = (None, *refs) if first else refs
    step = pl.program_id(0)

    @pl.when(step == 0)
    def _():
        total[...] = jnp.zeros(total.shape, jnp.float32) if first else base_ref[...]

    total[...] += jnp.dot(term_ref[0], weight_ref[...], preferred_element_type=jnp.float32)

    @pl.when(step == pl.num_programs(0) - 1)
    def _():
        out_ref[...] = total[...].astype(out_ref.dtype)


def project(at, terms, weight, column_entry, base):
    groups, rows, wide = terms.shape
    first = base is None
    columns = weight.shape[1] // (lax.axis_size("head") if first else 1)
    whole = pl.BlockSpec((rows, columns), lambda s, at: (0, 0))
    return pl.pallas_call(
        functools.partial(project_body, first),
        out_shape=jax.ShapeDtypeStruct((rows, columns), jnp.float32 if first else jnp.bfloat16),
        grid_spec=pltpu.PrefetchScalarGridSpec(
            num_scalar_prefetch=1,
            grid=(groups,),
            in_specs=[
                pl.BlockSpec((1, rows, wide), lambda s, at: (s, 0, 0)),
                pl.BlockSpec((wide, columns), lambda s, at: (at[2 + s], at[column_entry] if first else 0)),
            ]
            + ([] if first else [whole]),
            out_specs=whole,
            scratch_shapes=[pltpu.VMEM((rows, columns), jnp.float32)],
        ),
        compiler_params=pltpu.CompilerParams(vmem_limit_bytes=40 * 1024 * 1024),
        cost_estimate=pl.CostEstimate(
            flops=2 * groups * rows * wide * columns,
            bytes_accessed=2 * groups * wide * columns + 6 * rows * columns,
            transcendentals=0,
        ),
    )(at, terms, weight, *([] if first else [base]))


def by_heads(groups, queries, keys, values, kv_tiles, tile_order, out_weight):
    n = lax.axis_size("seq")
    sub = n // groups
    me = lax.axis_index("seq")
    plane, inner = me // sub, me % sub
    bits = []
    bit = sub // 2
    while bit:
        bits.append(bit)
        bit //= 2
    head = lax.axis_index("head")
    at = jnp.stack([plane, inner] + [(plane + o) % groups for o in range(groups)] + [head])
    at = at.astype(jnp.int32)

    def slot_of_row(first, row, at):
        return lax.rem(at[0] - first - 2 * row + groups, groups) * sub + at[1]

    def place_of_slot(slot, at):
        from_plane = lax.div(slot, sub)
        place = lax.rem(at[0] - from_plane + groups, groups)
        for stage, bit in enumerate(bits):
            differs = lax.rem(lax.div(slot, bit) + lax.div(at[1], bit), 2)
            place += differs * (groups << stage)
        return place

    columns = out_weight.shape[1] // lax.axis_size("head")
    q, k, v, w_far = exchange(groups, bits, queries, keys, values, out_weight, columns)

    def plane_shift(x, by):
        return lax.ppermute(
            x, "seq", [(i, (i // sub + by) % groups * sub + i % sub) for i in range(n)]
        )

    pieces, far = [None] * groups, [None] * groups

    def attend(first, tiles, q):
        rows_of = functools.partial(slot_of_row, first)
        found = attention(q, k, v, at, kv_tiles, tile_order, rows_of, place_of_slot, first, tiles)
        return [found[i] for i in range(tiles)]

    def send_home(which, found):
        for o, piece in zip(which, found):
            pieces[o] = plane_shift(piece, -o)

    def to_far(which):
        for o in which:
            far[o] = lax.ppermute(pieces[o], "head", [(0, 1), (1, 0)])

    early, middle = list(range(1, groups, 2)), list(range(2, groups, 2))
    send_home(early, attend(1, len(early), q))
    if middle:
        found = attend(2, len(middle), q)
        held, found, q = lax.optimization_barrier(([pieces[o] for o in early], found, q))
        for o, piece in zip(early, held):
            pieces[o] = piece
        send_home(middle, found)
    to_far(early)
    pieces[0] = attend(0, 1, q)[0]
    held, pieces[0] = lax.optimization_barrier(([far[o] for o in early], pieces[0]))
    for o, piece in zip(early, held):
        far[o] = piece
    for o in middle:
        pieces[o], pieces[0] = lax.optimization_barrier((pieces[o], pieces[0]))
    to_far([0, *middle])
    half_way = project(at, jnp.stack(pieces), out_weight, 2 + groups, None)
    return project(at, jnp.stack(far), w_far, None, half_way)


def per_device(queries, keys, values, kv_tiles, tile_order, out_weight):
    n = lax.axis_size("seq")
    groups = math.gcd(queries.shape[1] // HEAD_DIM, n)
    sub = n // groups
    power_of_two = sub & (sub - 1) == 0
    two_groups = lax.axis_size("head") == 2
    if two_groups and groups > 1 and sub > 1 and power_of_two and n <= 2 * (2 * REACH + 1):
        return by_heads(groups, queries, keys, values, kv_tiles, tile_order, out_weight)
    return by_ring(queries, keys, values, kv_tiles, tile_order, out_weight)


def solution(mesh):
    return jax.shard_map(
        per_device,
        mesh=mesh,
        in_specs=(P("seq", "head"), P("seq", "head"), P("seq", "head"), P(), P(), P("head", None)),
        out_specs=P("seq", "head"),
        check_vma=False,
    )
```

```python
import functools
import math

import jax
import jax.numpy as jnp
from jax import lax
from jax.experimental import pallas as pl
from jax.experimental.pallas import tpu as pltpu
from jax.sharding import PartitionSpec as P

HEAD_DIM = 128
REACH = 6
MESH = pl.DeviceIdType.MESH


def attention_body(
    slot_of_row, place_of_slot, at_ref, tiles_ref, order_ref, q_ref, k_ref, v_ref, out_ref, scores, tops, summed
):
    slots, width = tiles_ref.shape
    at = [at_ref[i] for i in range(at_ref.shape[0])]
    first_tile = order_ref[0]
    own_tile = order_ref[slot_of_row(pl.program_id(0), at)]
    count = 0
    for entry in range(width):
        count += jnp.where(tiles_ref[own_tile, entry] >= 0, 1, 0)

    def place_at(entry):
        slot = lax.rem(tiles_ref[own_tile, entry] - first_tile + slots, slots)
        return place_of_slot(slot, at)

    heads = q_ref.shape[0]
    scale = math.log2(math.e) / math.sqrt(HEAD_DIM)
    tops[...] = jnp.full(tops.shape, -jnp.inf, jnp.float32)
    summed[...] = jnp.zeros(summed.shape, jnp.float32)
    ones = jnp.ones((k_ref.shape[2], HEAD_DIM), jnp.bfloat16)

    def find(entry, carry):
        place = place_at(entry)
        for h in range(heads):
            fresh = lax.dot_general(
                q_ref[h, 0],
                k_ref[h, place],
                (((1,), (1,)), ((), ())),
                preferred_element_type=jnp.float32,
            )
            scores[h, entry] = fresh
            best = tops[h]
            for lane in range(0, fresh.shape[1], HEAD_DIM):
                best = jnp.maximum(best, fresh[:, lane : lane + HEAD_DIM])
            tops[h] = best
        return carry

    lax.fori_loop(0, count, find, 0)
    for h in range(heads):
        top = jnp.max(tops[h], axis=1, keepdims=True) * scale
        tops[h] = jnp.broadcast_to(top, tops.shape[1:])

    def add(entry, carry):
        place = place_at(entry)
        for h in range(heads):
            top = tops[h]
            weights = jnp.concatenate(
                [
                    jnp.exp2(scores[h, entry, :, lane : lane + HEAD_DIM] * scale - top).astype(jnp.bfloat16)
                    for lane in range(0, scores.shape[3], HEAD_DIM)
                ],
                axis=1,
            )
            paired = jnp.concatenate([v_ref[h, place], ones], axis=1)
            summed[h] += jnp.dot(weights, paired, preferred_element_type=jnp.float32)
        return carry

    lax.fori_loop(0, count, add, 0)
    for h in range(heads):
        done = summed[h]
        out_ref[0, :, h * HEAD_DIM : (h + 1) * HEAD_DIM] = (
            done[:, :HEAD_DIM] / done[:, HEAD_DIM:]
        ).astype(jnp.bfloat16)


def attention(q, k, v, at, kv_tiles, tile_order, slot_of_row, place_of_slot, first, tiles):
    heads, _, rows, _ = q.shape
    key_tiles = k.shape[1]
    width = kv_tiles.shape[1]
    units = heads * tiles * min(width, key_tiles)
    key_spec = pl.BlockSpec(
        (heads, key_tiles, rows, HEAD_DIM), lambda t, *_: (0, 0, 0, 0), pipeline_mode=pl.Buffered(1)
    )
    return pl.pallas_call(
        functools.partial(attention_body, slot_of_row, place_of_slot),
        out_shape=jax.ShapeDtypeStruct((tiles, rows, heads * HEAD_DIM), jnp.bfloat16),
        grid_spec=pltpu.PrefetchScalarGridSpec(
            num_scalar_prefetch=3,
            grid=(tiles,),
            in_specs=[
                pl.BlockSpec((heads, 1, rows, HEAD_DIM), lambda t, *_: (0, first + 2 * t, 0, 0)),
                key_spec,
                key_spec,
            ],
            out_specs=pl.BlockSpec((1, rows, heads * HEAD_DIM), lambda t, *_: (t, 0, 0)),
            scratch_shapes=[
                pltpu.VMEM((heads, width, rows, rows), jnp.float32),
                pltpu.VMEM((heads, rows, HEAD_DIM), jnp.float32),
                pltpu.VMEM((heads, rows, 2 * HEAD_DIM), jnp.float32),
            ],
        ),
        compiler_params=pltpu.CompilerParams(vmem_limit_bytes=52 * 1024 * 1024),
        cost_estimate=pl.CostEstimate(
            flops=units * rows * rows * HEAD_DIM * 4,
            bytes_accessed=2 * (2 * q.size + k.size + v.size),
            transcendentals=units * rows * rows,
        ),
    )(at, kv_tiles, tile_order, q, k, v)


def by_ring(queries, keys, values, kv_tiles, tile_order, out_weight):
    rows, local_width = queries.shape
    heads = local_width // HEAD_DIM
    n = lax.axis_size("seq")
    me = lax.axis_index("seq")
    window = 2 * REACH + 1
    pair = jnp.stack([keys, values])
    received = {0: pair}
    for heading in (1, -1):
        moving = pair
        for stride in range(1, REACH + 1):
            moving = lax.ppermute(moving, "seq", [(i, (i + heading) % n) for i in range(n)])
            received[-heading * stride] = moving
    both = jnp.stack([received[o] for o in range(-REACH, REACH + 1)])
    both = both.reshape(window, 2, rows, heads, HEAD_DIM).transpose(1, 3, 0, 2, 4)
    q = queries.reshape(rows, heads, HEAD_DIM).transpose(1, 0, 2)[:, None]
    attended = attention(
        q,
        both[0],
        both[1],
        me.reshape(1).astype(jnp.int32),
        kv_tiles,
        tile_order,
        lambda row, at: at[0],
        lambda slot, at: lax.rem(slot - at[0] + REACH + n, n),
        0,
        1,
    )[0]
    partial = jnp.dot(attended, out_weight, preferred_element_type=jnp.float32).astype(jnp.bfloat16)
    return lax.psum_scatter(partial, "head", scatter_dimension=1, tiled=True)


def exchange_body(
    groups, share, bits, q_ref, k_ref, v_ref, w_ref, q_out, k_out, v_out, w_out,
    local_sem, plane_send, plane_recv, swap_send, swap_recv, w_send, w_recv,
):
    sub = lax.axis_size("seq") // groups
    me = lax.axis_index("seq")
    plane, inner = me // sub, me % sub
    other = 1 - lax.axis_index("head")

    def across(o):
        return {"seq": (plane + o) % groups * sub + inner}

    def swapped(bit):
        return {"seq": plane * sub + inner + bit * (1 - 2 * (inner // bit % 2))}

    partners = [across(o) for o in range(1, groups)] + [swapped(b) for b in bits] + [{"head": other}]
    barrier = pltpu.get_barrier_semaphore()
    for partner in partners:
        pl.semaphore_signal(barrier, inc=1, device_id=partner, device_id_type=MESH)
    pl.semaphore_wait(barrier, len(partners))

    half = w_ref.shape[0] // 2
    columns = w_out.shape[1]
    own_rows = pl.ds(pl.multiple_of(me % 2 * half, half), half)
    w_cross = pltpu.make_async_remote_copy(
        src_ref=w_ref.at[own_rows, pl.ds(pl.multiple_of(other * columns, columns), columns)],
        dst_ref=w_out.at[own_rows],
        send_sem=w_send.at[0],
        recv_sem=w_recv.at[0],
        device_id={"head": other},
        device_id_type=MESH,
    )
    w_cross.start()
    arrays = ((k_ref, k_out), (v_ref, v_out), (q_ref, q_out))

    def cut(ref, to_plane, j):
        start = (to_plane * share + j) * HEAD_DIM
        return ref.at[:, pl.ds(pl.multiple_of(start, HEAD_DIM), HEAD_DIM)]

    local, crossing = {}, {}
    for j, a in [(j, a) for j in range(share) for a in (0, 1)] + [(j, 2) for j in range(share)]:
        src, dst = arrays[a]
        for o in range(1, groups):
            crossing[j, o, a] = pltpu.make_async_remote_copy(
                src_ref=cut(src, (plane + o) % groups, j),
                dst_ref=dst.at[j, o],
                send_sem=plane_send.at[j, o, a],
                recv_sem=plane_recv.at[j, o, a],
                device_id=across(o),
                device_id_type=MESH,
            )
            crossing[j, o, a].start()
        local[j, a] = pltpu.make_async_copy(cut(src, plane, j), dst.at[j, 0], local_sem.at[j, a])
        local[j, a].start()

    swaps = {}

    def start_swap(j, stage):
        held = groups << stage
        for a in range(2):
            out = arrays[a][1]
            swaps[j, stage, a] = pltpu.make_async_remote_copy(
                src_ref=out.at[j, pl.ds(0, held)],
                dst_ref=out.at[j, pl.ds(held, held)],
                send_sem=swap_send.at[j, stage, a],
                recv_sem=swap_recv.at[j, stage, a],
                device_id=swapped(bits[stage]),
                device_id_type=MESH,
            )
            swaps[j, stage, a].start()

    for step in range(share + len(bits)):
        for stage in range(min(step, len(bits)), -1, -1):
            j = step - stage
            if not 0 <= j < share:
                continue
            for a in range(2):
                if stage == 0:
                    local[j, a].wait()
                    for o in range(1, groups):
                        crossing[j, o, a].wait_recv()
                else:
                    swaps[j, stage - 1, a].wait_recv()
            if stage < len(bits):
                start_swap(j, stage)
        if step == share - 1:
            w_cross.wait_recv()
            w_on = pltpu.make_async_remote_copy(
                src_ref=w_out.at[own_rows],
                dst_ref=w_out.at[own_rows],
                send_sem=w_send.at[1],
                recv_sem=w_recv.at[1],
                device_id=swapped(1),
                device_id_type=MESH,
            )
            w_on.start()
    for j in range(share):
        local[j, 2].wait()
        for o in range(1, groups):
            crossing[j, o, 2].wait_recv()
            for a in range(3):
                crossing[j, o, a].wait_send()
        for stage in range(len(bits)):
            for a in range(2):
                swaps[j, stage, a].wait_send()
    w_cross.wait_send()
    w_on.wait()


def exchange(groups, bits, queries, keys, values, out_weight, columns):
    rows, local_width = queries.shape
    share = local_width // HEAD_DIM // groups
    n = lax.axis_size("seq")
    anywhere = pl.BlockSpec(memory_space=pl.ANY)
    kind = jnp.bfloat16
    stages = len(bits)
    return pl.pallas_call(
        functools.partial(exchange_body, groups, share, bits),
        out_shape=(
            jax.ShapeDtypeStruct((share, groups, rows, HEAD_DIM), kind),
            jax.ShapeDtypeStruct((share, n, rows, HEAD_DIM), kind),
            jax.ShapeDtypeStruct((share, n, rows, HEAD_DIM), kind),
            jax.ShapeDtypeStruct((out_weight.shape[0], columns), kind),
        ),
        in_specs=[anywhere] * 4,
        out_specs=(anywhere,) * 4,
        scratch_shapes=[
            pltpu.SemaphoreType.DMA((share, 3)),
            pltpu.SemaphoreType.DMA((share, groups, 3)),
            pltpu.SemaphoreType.DMA((share, groups, 3)),
            pltpu.SemaphoreType.DMA((share, stages, 2)),
            pltpu.SemaphoreType.DMA((share, stages, 2)),
            pltpu.SemaphoreType.DMA((2,)),
            pltpu.SemaphoreType.DMA((2,)),
        ],
        compiler_params=pltpu.CompilerParams(collective_id=0, has_side_effects=True),
    )(queries, keys, values, out_weight)


def project_body(first, at_ref, term_ref, weight_ref, *refs):
    base_ref, out_ref, total = (None, *refs) if first else refs
    step = pl.program_id(0)

    @pl.when(step == 0)
    def _():
        total[...] = jnp.zeros(total.shape, jnp.float32) if first else base_ref[...]

    total[...] += jnp.dot(term_ref[0], weight_ref[...], preferred_element_type=jnp.float32)

    @pl.when(step == pl.num_programs(0) - 1)
    def _():
        out_ref[...] = total[...].astype(out_ref.dtype)


def project(at, terms, weight, column_entry, base, start=0, step=1, kind=jnp.float32):
    groups, rows, wide = terms.shape
    first = base is None
    columns = weight.shape[1] // (lax.axis_size("head") if first else 1)
    whole = pl.BlockSpec((rows, columns), lambda s, at: (0, 0))
    return pl.pallas_call(
        functools.partial(project_body, first),
        out_shape=jax.ShapeDtypeStruct((rows, columns), kind),
        grid_spec=pltpu.PrefetchScalarGridSpec(
            num_scalar_prefetch=1,
            grid=(groups,),
            in_specs=[
                pl.BlockSpec((1, rows, wide), lambda s, at: (s, 0, 0)),
                pl.BlockSpec((wide, columns), lambda s, at: (at[2 + start + step * s], at[column_entry] if first else 0)),
            ]
            + ([] if first else [whole]),
            out_specs=whole,
            scratch_shapes=[pltpu.VMEM((rows, columns), jnp.float32)],
        ),
        compiler_params=pltpu.CompilerParams(vmem_limit_bytes=40 * 1024 * 1024),
        cost_estimate=pl.CostEstimate(
            flops=2 * groups * rows * wide * columns,
            bytes_accessed=2 * groups * wide * columns + 6 * rows * columns,
            transcendentals=0,
        ),
    )(at, terms, weight, *([] if first else [base]))


def by_heads(groups, queries, keys, values, kv_tiles, tile_order, out_weight):
    n = lax.axis_size("seq")
    sub = n // groups
    me = lax.axis_index("seq")
    plane, inner = me // sub, me % sub
    bits = []
    bit = sub // 2
    while bit:
        bits.append(bit)
        bit //= 2
    head = lax.axis_index("head")
    at = jnp.stack([plane, inner] + [(plane + o) % groups for o in range(groups)] + [head])
    at = at.astype(jnp.int32)

    def slot_of_row(first, row, at):
        return lax.rem(at[0] - first - 2 * row + groups, groups) * sub + at[1]

    def place_of_slot(slot, at):
        from_plane = lax.div(slot, sub)
        place = lax.rem(at[0] - from_plane + groups, groups)
        for stage, bit in enumerate(bits):
            differs = lax.rem(lax.div(slot, bit) + lax.div(at[1], bit), 2)
            place += differs * (groups << stage)
        return place

    columns = out_weight.shape[1] // lax.axis_size("head")
    q, k, v, w_far = exchange(groups, bits, queries, keys, values, out_weight, columns)

    def plane_shift(x, by):
        return lax.ppermute(
            x, "seq", [(i, (i // sub + by) % groups * sub + i % sub) for i in range(n)]
        )

    pieces, far = [None] * groups, [None] * groups

    def attend(first, tiles, q):
        rows_of = functools.partial(slot_of_row, first)
        found = attention(q, k, v, at, kv_tiles, tile_order, rows_of, place_of_slot, first, tiles)
        return [found[i] for i in range(tiles)]

    def send_home(which, found):
        for o, piece in zip(which, found):
            pieces[o] = plane_shift(piece, -o)

    def to_far(which):
        for o in which:
            far[o] = lax.ppermute(pieces[o], "head", [(0, 1), (1, 0)])

    early, middle = list(range(1, groups, 2)), list(range(2, groups, 2))
    send_home(early, attend(1, len(early), q))
    if middle:
        found = attend(2, len(middle), q)
        held, found, q = lax.optimization_barrier(([pieces[o] for o in early], found, q))
        for o, piece in zip(early, held):
            pieces[o] = piece
        send_home(middle, found)
    to_far(early)
    pieces[0] = attend(0, 1, q)[0]
    held, pieces[0] = lax.optimization_barrier(([far[o] for o in early], pieces[0]))
    for o, piece in zip(early, held):
        far[o] = piece
    for o in middle:
        pieces[o], pieces[0] = lax.optimization_barrier((pieces[o], pieces[0]))
    to_far([0, *middle])
    half_way = project(at, jnp.stack(pieces), out_weight, 2 + groups, None)
    nearly = project(at, jnp.stack([far[o] for o in early]), w_far, None, half_way, 1, 2)
    late = jnp.stack([far[o] for o in [0, *middle]])
    return project(at, late, w_far, None, nearly, 0, 2, jnp.bfloat16)


def per_device(queries, keys, values, kv_tiles, tile_order, out_weight):
    n = lax.axis_size("seq")
    groups = math.gcd(queries.shape[1] // HEAD_DIM, n)
    sub = n // groups
    power_of_two = sub & (sub - 1) == 0
    two_groups = lax.axis_size("head") == 2
    if two_groups and groups > 1 and sub > 1 and power_of_two and n <= 2 * (2 * REACH + 1):
        return by_heads(groups, queries, keys, values, kv_tiles, tile_order, out_weight)
    return by_ring(queries, keys, values, kv_tiles, tile_order, out_weight)


def solution(mesh):
    return jax.shard_map(
        per_device,
        mesh=mesh,
        in_specs=(P("seq", "head"), P("seq", "head"), P("seq", "head"), P(), P(), P("head", None)),
        out_specs=P("seq", "head"),
        check_vma=False,
    )
```
